512 devices in a mesh: row: 16 (over x, y), col: 8 (over z_lo, core), dep: 4 (over z_hi).
Axes of the slice: x: 4, y: 4, z: 16 (z_hi: 4, z_lo: 4; z = z_hi * 4 + z_lo), core: 2. Of those that a mesh axis runs over, the one named last changes fastest.
Arguments:
- inputs: bfloat16 [1536, 8192], P(('dep', 'col'), 'row'), may hold values from -6 to 6
- gate_weight: bfloat16 [8192, 14336], P('row', 'col'), may hold values from -0.0625 to 0.0625
- up_weight: bfloat16 [8192, 14336], P('row', 'col'), may hold values from -0.0625 to 0.0625
- cotangent: bfloat16 [1536, 14336], P(('dep', 'row'), 'col'), may hold values from -6 to 6
Outputs:
- input_grad: bfloat16 [1536, 8192], P(('dep', 'col'), 'row')
- gate_weight_grad: bfloat16 [8192, 14336], P(('row', 'dep'), 'col')
- up_weight_grad: bfloat16 [8192, 14336], P(('row', 'dep'), 'col')
The draws below stay inside these ranges and needn't reach their ends.
All inputs are finite; a program needn't handle non-finite values.
Results may differ from the reference program's by a relative error of at most 0.029.
Values may be sent and summed in bfloat16 or wider, within the bound.
A program may use at most 64 MiB of HBM per device.

```python
import math
import jax
import jax.numpy as jnp
from jax import lax

D = 8192
FF = 14336
TOKENS = 1536
N_ROW = 16
N_COL = 8
N_DEP = 4


def steps_of(stream_key, dims, split, low, largest):
    def one(position, parts):
        heights = jax.random.uniform(jax.random.fold_in(jax.random.fold_in(stream_key, 6), position), (parts,), jnp.float32, low / len(split), largest / len(split))
        return jnp.repeat(jnp.exp(heights), dims[position] // parts).reshape((-1,) + (1,) * (len(dims) - position - 1))

    level = one(*split[0])
    for cut in split[1:]:
        level = level * one(*cut)
    return level


def normal_values(stream_key, extent, spread, limit, cuts=(), held_as=jnp.bfloat16):
    array = jax.random.normal(stream_key, extent, jnp.float32) * spread
    if len(cuts) > 0:
        array = steps_of(stream_key, extent, cuts, -0.22, 0.18) * array
    return jnp.clip(array, min=-limit, max=limit).astype(held_as)


def setup_inputs(seed: int = 0) -> dict:
    keys = jax.random.split(jax.random.key(seed), 5)
    return {
        "inputs": normal_values(keys[0], (TOKENS, D), 1.0, 6.0, ((0, 32), (1, 16))),
        "gate_weight": normal_values(keys[1], (D, FF), D ** -0.5, 0.0625, ((0, 16), (1, 8))),
        "up_weight": normal_values(keys[2], (D, FF), D ** -0.5, 0.0625, ((0, 16), (1, 8))),
        "cotangent": normal_values(keys[3], (TOKENS, FF), 1.0, 6.0, ((0, 64), (1, 8))),
    }


def rounded(values):
    return lax.optimization_barrier(values.astype(jnp.bfloat16)).astype(jnp.float32)

def reference(inputs, gate_weight, up_weight, cotangent):
    feature_width = D // N_ROW
    hidden_width = FF // N_COL
    group_tokens = TOKENS // N_DEP
    gate_sum = jnp.zeros((TOKENS, FF), jnp.float32)
    up_sum = jnp.zeros((TOKENS, FF), jnp.float32)
    for shard_row in range(N_ROW):
        lower = shard_row * feature_width
        columns = inputs[:, lower:lower + feature_width]
        gate_sum = gate_sum + rounded(jnp.dot(columns, gate_weight[lower:lower + feature_width], preferred_element_type=jnp.float32))
        up_sum = up_sum + rounded(jnp.dot(columns, up_weight[lower:lower + feature_width], preferred_element_type=jnp.float32))
    gate_sig = jax.nn.sigmoid(gate_sum)
    cot_wide = cotangent.astype(jnp.float32)
    grad_gate = (cot_wide * up_sum * gate_sig * (1.0 + gate_sum * (1.0 - gate_sig))).astype(jnp.bfloat16)
    grad_up = (cot_wide * gate_sum * gate_sig).astype(jnp.bfloat16)
    input_total = jnp.zeros((TOKENS, D), jnp.float32)
    for shard_col in range(N_COL):
        lower = shard_col * hidden_width
        upper = lower + hidden_width
        term = jnp.dot(grad_gate[:, lower:upper], gate_weight[:, lower:upper].T, preferred_element_type=jnp.float32)
        term = term + jnp.dot(grad_up[:, lower:upper], up_weight[:, lower:upper].T, preferred_element_type=jnp.float32)
        input_total = input_total + rounded(term)
    loss_scale = 1.0 / math.sqrt(TOKENS)
    gate_total = jnp.zeros((D, FF), jnp.float32)
    up_total = jnp.zeros((D, FF), jnp.float32)
    for quarter in range(N_DEP):
        lower = quarter * group_tokens
        upper = lower + group_tokens
        rows_in = inputs[lower:upper].T
        gate_total = gate_total + rounded(loss_scale * jnp.dot(rows_in, grad_gate[lower:upper], preferred_element_type=jnp.float32))
        up_total = up_total + rounded(loss_scale * jnp.dot(rows_in, grad_up[lower:upper], preferred_element_type=jnp.float32))
    return (input_total.astype(jnp.bfloat16), gate_total.astype(jnp.bfloat16), up_total.astype(jnp.bfloat16))
```

```python
import math

import jax
import jax.numpy as jnp
from jax import lax
from jax.experimental import pallas as pl
from jax.experimental.pallas import tpu as pltpu
from jax.sharding import PartitionSpec as P

MESH = pl.DeviceIdType.MESH
F32 = jnp.float32
BF16 = jnp.bfloat16

OFFSETS = (0, 1, 3, 2)
HALF = 896
BLOCK = 48
TILES = ((0, 256), (256, 256), (512, 256), (768, 128))
CHANNELS = 176


def dot(left, right, dims):
    return lax.dot_general(left, right, (dims, ((), ())), preferred_element_type=F32)


def kernel(
    x_in, wg_hbm, wu_hbm, cot,
    ig_out, gate_out, up_out,
    wg, wu, xp, xw, sa, sb, ra, rb, ta, tb, rta, rtb, cf, cb, grads, acc, igs, igr,
    send_sem, recv_sem, local_sem,
):
    row, col, dep = lax.axis_index("row"), lax.axis_index("col"), lax.axis_index("dep")
    x, y = row // 4, row % 4
    zl, core = col // 2, col % 2
    half = (x + y) % 2
    bit = y % 2

    loads = [
        pltpu.make_async_copy(wg_hbm, wg, local_sem.at[0]),
        pltpu.make_async_copy(wu_hbm, wu, local_sem.at[1]),
    ]
    for load in loads:
        load.start()

    def at_x(step):
        return (((x + step) % 4) * 4 + y, col, dep)

    def at_y(step):
        return (x * 4 + (y + step) % 4, col, dep)

    def at_dep(step):
        return (row, col, (dep + step) % 4)

    def at_col(step):
        return (row, (col + step) % 8, dep)

    sibling = (row, zl * 2 + 1 - core, dep)

    barrier = pltpu.get_barrier_semaphore()
    partners = (
        [at_x(s) for s in (1, 2, 3)]
        + [at_y(s) for s in (1, 2, 3)]
        + [at_dep(s) for s in (1, 2, 3)]
        + [at_col(s) for s in range(1, 8)]
    )
    for partner in partners:
        pl.semaphore_signal(barrier, inc=1, device_id=partner, device_id_type=MESH)
    pl.semaphore_wait(barrier, len(partners))

    pending = []
    used = {}

    def channel(name):
        if name not in used:
            used[name] = len(used)
        assert len(used) <= CHANNELS
        return used[name]

    def copy(name, src, dst, device):
        i = channel(name)
        return pltpu.make_async_remote_copy(
            src_ref=src, dst_ref=dst, send_sem=send_sem.at[i], recv_sem=recv_sem.at[i],
            device_id=device, device_id_type=MESH,
        )

    def send(name, src, dst, device):
        c = copy(name, src, dst, device)
        c.start()
        pending.append(c)

    def recv(name, dst):
        copy(name, dst, dst, sibling).wait_recv()

    def slot(step, which):
        return ((zl + 4 - step) % 4) * 2 + which

    for s in (1, 2, 3):
        send(("x", s), x_in, xp.at[col], (row, ((zl + s) % 4) * 2 + core, dep))
    send("xs", x_in, xp.at[col], sibling)
    xp[col] = x_in[...]

    wide = cot[...].astype(F32)
    cf[0] = wide[:, :HALF]
    cf[1] = wide[:, HALF:]
    cb[bit] = cf[half]
    send("cot", cf.at[1 - half], cb.at[bit], (x * 4 + y + 1 - 2 * bit, col, dep))

    for s in (1, 3, 2):
        here = xp.at[slot(s, core)]
        recv(("x", s), here)
        send(("xf", s), here, here, sibling)
    recv("xs", xp.at[slot(0, 1 - core)])
    for s in (1, 3, 2):
        recv(("xf", s), xp.at[slot(s, 1 - core)])

    panel = xp[...].reshape(8 * BLOCK, 512)
    for load in loads:
        load.wait()
    paths = ((sa, ra, at_x, x), (sb, rb, at_y, y))
    for h in (0, 1):
        for part, weight in ((0, wg), (1, wu)):
            for lower, width in TILES:
                term = dot(panel, weight[:, HALF * h + lower : HALF * h + lower + width], ((1,), (0,)))
                term = term.astype(BF16)
                for k in range(8):
                    rows = term[BLOCK * k : BLOCK * k + BLOCK]
                    bx, j = k // 2, k % 2
                    if part == 0:
                        sa[bx, h, j, :, lower : lower + width] = rows
                    else:
                        by = 2 * j + (h + bx) % 2
                        sb[by, h, bx // 2, :, lower : lower + width] = rows
            src, dst, at, pos = paths[part]
            toward = 3 if h == 0 else 1
            far = (pos + 2) % 4
            send(("opp", part, h), src.at[far, h], dst.at[0, h], at(toward))
            back = 4 - toward
            send(("dir", part, h), src.at[(pos + back) % 4, h], dst.at[1, h], at(back))

    for s in (1, 3, 2):
        e = OFFSETS.index(4 - s)
        theirs = pl.ds(pl.multiple_of(((dep + s) % 4) * 128, 128), 128)
        send(("xw", e), xp.at[:, :, theirs], xw.at[e], at_dep(s))
    mine = pl.ds(pl.multiple_of(dep * 128, 128), 128)
    xw[0] = xp[:, :, mine]

    for h in (0, 1):
        for part in (0, 1):
            src, dst, at, pos = paths[part]
            toward = 3 if h == 0 else 1
            target = (pos + toward) % 4
            recv(("opp", part, h), dst.at[0, h])
            src[target, h] = (src[target, h].astype(F32) + dst[0, h].astype(F32)).astype(BF16)
            send(("acc", part, h), src.at[target, h], dst.at[2, h], at(toward))

    second = ((ta, rta, at_y, y), (tb, rtb, at_x, x))
    for part in (0, 1):
        src, dst, at, pos = paths[part]
        t, rt, at2, pos2 = second[part]
        for h in (0, 1):
            recv(("dir", part, h), dst.at[1, h])
            recv(("acc", part, h), dst.at[2, h])
            for j in (0, 1):
                total = (
                    src[pos, h, j].astype(F32) + dst[1, h, j].astype(F32) + dst[2, h, j].astype(F32)
                )
                t[2 * j + (h + pos) % 2] = total.astype(BF16)
        for s in (1, 3, 2):
            send(("two", part, s), t.at[(pos2 + s) % 4], rt.at[s - 1], at2(s))
    sums = []
    for part in (0, 1):
        t, rt, at2, pos2 = second[part]
        total = t[pos2].astype(F32)
        for s in (1, 3, 2):
            recv(("two", part, s), rt.at[s - 1])
            total = total + rt[s - 1].astype(F32)
        sums.append(total)
    gate_sum, up_sum = sums

    recv("cot", cb.at[1 - bit])
    cot_wide = cb[...].reshape(BLOCK, HALF)
    gate_sig = jax.nn.sigmoid(gate_sum)
    khi, klo = x // 2, 2 * (x % 2) + y // 2
    grads[0, 0, half, khi, klo] = (
        cot_wide * up_sum * gate_sig * (1.0 + gate_sum * (1.0 - gate_sig))
    ).astype(BF16)
    grads[0, 1, half, khi, klo] = (cot_wide * gate_sum * gate_sig).astype(BF16)

    for s in (1, 3, 2):
        e = OFFSETS.index(4 - s)
        for part in (0, 1):
            send(
                ("z", part, e),
                grads.at[0, part, half, khi, klo],
                grads.at[e, part, half, khi, klo],
                at_dep(s),
            )

    def own(e, part):
        return grads.at[e, part, half, khi, klo]

    def chunk(e, part, h, step):
        if part == 0:
            px = (x + step) % 4
            return grads.at[e, 0, h, px // 2, pl.ds(2 * (px % 2), 2)]
        py = (y + step) % 4
        return grads.at[e, 1, h, :, 2 * ((h + py) % 2) + py // 2]

    ring_one = (at_y, at_x)
    ring_two = (at_x, at_y)

    def start_first(e):
        for part in (0, 1):
            if e > 0:
                recv(("z", part, e), own(e, part))
            for s in (1, 3, 2):
                send(("g1", e, part, s), own(e, part), own(e, part), ring_one[part](s))

    def start_second(e):
        for part in (0, 1):
            at = ring_two[part]
            for s in (1, 3, 2):
                recv(("g1", e, part, s), own(e, part))
            for h in (0, 1):
                c = chunk(e, part, h, 0)
                send(("g2", e, part, 1, h), c, c, at(1))
                c = chunk(e, part, 1 - h, 0)
                send(("g2", e, part, 3, 1 - h), c, c, at(3))

    def relay(e):
        for part in (0, 1):
            at = ring_two[part]
            for s, h in ((1, 0), (3, 1)):
                c = chunk(e, part, h, 4 - s)
                recv(("g2", e, part, s, h), c)
                send(("g3", e, part, h), c, c, at(s))

    def finish(e):
        for part in (0, 1):
            for s, h in ((1, 1), (3, 0)):
                recv(("g2", e, part, s, h), chunk(e, part, h, 4 - s))
            for h in (0, 1):
                recv(("g3", e, part, h), chunk(e, part, h, 2))

    def weight_grads(e):
        if e > 0:
            recv(("xw", e), xw.at[e])
        features = xw[e].reshape(8 * BLOCK, 128)
        for part in (0, 1):
            for h in (0, 1):
                block = grads[e, part, h].reshape(8 * BLOCK, HALF)
                term = dot(features, block, ((0,), (0,)))
                if e == 0:
                    acc[part, h] = term
                else:
                    acc[part, h] += term

    def input_grad():
        total = None
        for part, weight in ((0, wg), (1, wu)):
            for h in (0, 1):
                block = grads[0, part, h].reshape(8 * BLOCK, HALF)
                term = dot(block, weight[:, HALF * h : HALF * h + HALF], ((1,), (1,)))
                total = term if total is None else total + term
        igs[...] = total.astype(BF16).reshape(8, BLOCK, 512)
        for s in range(1, 8):
            send(("ig", s), igs.at[(col + s) % 8], igr.at[s - 1], at_col(s))

    start_first(0)
    start_second(0)
    relay(0)
    start_first(1)
    start_second(1)
    finish(0)
    input_grad()
    weight_grads(0)
    for e in (1, 2, 3):
        relay(e)
        if e < 3:
            start_first(e + 1)
            start_second(e + 1)
        finish(e)
        weight_grads(e)

    loss_scale = 1.0 / math.sqrt(4 * 8 * BLOCK)
    for part, out in ((0, gate_out), (1, up_out)):
        for h in (0, 1):
            out[:, HALF * h : HALF * h + HALF] = (loss_scale * acc[part, h]).astype(BF16)

    total = igs[col].astype(F32)
    for s in range(1, 8):
        recv(("ig", s), igr.at[s - 1])
        total = total + igr[s - 1].astype(F32)
    ig_out[...] = total.astype(BF16)

    for c in pending:
        c.wait_send()


def local(inputs, gate_weight, up_weight, cotangent):
    vmem = pl.BlockSpec(memory_space=pltpu.VMEM)
    hbm = pl.BlockSpec(memory_space=pl.ANY)
    return pl.pallas_call(
        kernel,
        name="swiglu_backward",
        out_shape=(
            jax.ShapeDtypeStruct((48, 512), BF16),
            jax.ShapeDtypeStruct((128, 1792), BF16),
            jax.ShapeDtypeStruct((128, 1792), BF16),
        ),
        in_specs=[vmem, hbm, hbm, vmem],
        out_specs=(vmem, vmem, vmem),
        scratch_shapes=[
            pltpu.VMEM((512, 1792), BF16),
            pltpu.VMEM((512, 1792), BF16),
            pltpu.VMEM((8, BLOCK, 512), BF16),
            pltpu.VMEM((4, 8, BLOCK, 128), BF16),
            pltpu.VMEM((4, 2, 2, BLOCK, HALF), BF16),
            pltpu.VMEM((4, 2, 2, BLOCK, HALF), BF16),
            pltpu.VMEM((3, 2, 2, BLOCK, HALF), BF16),
            pltpu.VMEM((3, 2, 2, BLOCK, HALF), BF16),
            pltpu.VMEM((4, BLOCK, HALF), BF16),
            pltpu.VMEM((4, BLOCK, HALF), BF16),
            pltpu.VMEM((3, BLOCK, HALF), BF16),
            pltpu.VMEM((3, BLOCK, HALF), BF16),
            pltpu.VMEM((2, 24, HALF), F32),
            pltpu.VMEM((2, 24, HALF), F32),
            pltpu.VMEM((4, 2, 2, 2, 4, BLOCK, HALF), BF16),
            pltpu.VMEM((2, 2, 128, HALF), F32),
            pltpu.VMEM((8, BLOCK, 512), BF16),
            pltpu.VMEM((7, BLOCK, 512), BF16),
            pltpu.SemaphoreType.DMA((CHANNELS,)),
            pltpu.SemaphoreType.DMA((CHANNELS,)),
            pltpu.SemaphoreType.DMA((2,)),
        ],
        compiler_params=pltpu.CompilerParams(
            collective_id=0, has_side_effects=True, vmem_limit_bytes=56 * 2**20
        ),
    )(inputs, gate_weight, up_weight, cotangent)


def solution(mesh):
    return jax.shard_map(
        local,
        mesh=mesh,
        in_specs=(
            P(("dep", "col"), "row"),
            P("row", "col"),
            P("row", "col"),
            P(("dep", "row"), "col"),
        ),
        out_specs=(P(("dep", "col"), "row"), P(("row", "dep"), "col"), P(("row", "dep"), "col")),
        check_vma=False,
    )
```

```python
import math

import jax
import jax.numpy as jnp
from jax import lax
from jax.experimental import pallas as pl
from jax.experimental.pallas import tpu as pltpu
from jax.sharding import PartitionSpec as P

MESH = pl.DeviceIdType.MESH
F32 = jnp.float32
BF16 = jnp.bfloat16

OFFSETS = (0, 1, 3, 2)
HALF = 896
BLOCK = 48
TILES = ((0, 256), (256, 256), (512, 256), (768, 128))
CHANNELS = 176


def dot(left, right, dims):
    return lax.dot_general(left, right, (dims, ((), ())), preferred_element_type=F32)


def kernel(
    x_in, wg_hbm, wu_hbm, cot,
    ig_out, gate_out, up_out,
    wg, wu, xp, xw, sa, sb, ra, rb, ta, tb, rta, rtb, cf, cb, near, others, acc, outs, fin, igs, igr,
    send_sem, recv_sem, local_sem,
):
    row, col, dep = lax.axis_index("row"), lax.axis_index("col"), lax.axis_index("dep")
    x, y = row // 4, row % 4
    zl, core = col // 2, col % 2
    half, part_here = y % 2, y // 2

    loads = [
        pltpu.make_async_copy(wg_hbm, wg, local_sem.at[0]),
        pltpu.make_async_copy(wu_hbm, wu, local_sem.at[1]),
    ]
    for load in loads:
        load.start()

    def at_x(step):
        return (((x + step) % 4) * 4 + y, col, dep)

    def at_y(step):
        return (x * 4 + (y + step) % 4, col, dep)

    def at_dep(step):
        return (row, col, (dep + step) % 4)

    def at_cross(step):
        return (x * 4 + (y + 2) % 4, col, (dep + step) % 4)

    def at_col(step):
        return (row, (col + step) % 8, dep)

    sibling = (row, zl * 2 + 1 - core, dep)

    barrier = pltpu.get_barrier_semaphore()
    partners = (
        [at_dep(s) for s in (2, 1, 3)]
        + [at_cross(s) for s in (1, 3)]
        + [at_col(s) for s in range(1, 8)]
        + [at_x(s) for s in (1, 2, 3)]
        + [at_y(s) for s in (1, 2, 3)]
    )
    for partner in partners:
        pl.semaphore_signal(barrier, inc=1, device_id=partner, device_id_type=MESH)
    wide = cot[...].astype(F32)
    cf[0] = wide[:, :HALF]
    cf[1] = wide[:, HALF:]
    cb[half] = cf[half]
    xp[col] = x_in[...]
    pl.semaphore_wait(barrier, len(partners))

    pending = []
    used = {}

    def channel(name):
        if name not in used:
            used[name] = len(used)
        assert len(used) <= CHANNELS
        return used[name]

    def copy(name, src, dst, device):
        i = channel(name)
        return pltpu.make_async_remote_copy(
            src_ref=src, dst_ref=dst, send_sem=send_sem.at[i], recv_sem=recv_sem.at[i],
            device_id=device, device_id_type=MESH,
        )

    def send(name, src, dst, device):
        c = copy(name, src, dst, device)
        c.start()
        pending.append(c)

    def recv(name, dst):
        copy(name, dst, dst, sibling).wait_recv()

    def slot(step, which):
        return ((zl + 4 - step) % 4) * 2 + which

    for s in (1, 2, 3):
        send(("x", s), x_in, xp.at[col], (row, ((zl + s) % 4) * 2 + core, dep))
    send("xs", x_in, xp.at[col], sibling)
    send("cot", cf.at[1 - half], cb.at[half], (x * 4 + y + 1 - 2 * half, col, dep))

    for s in (1, 3, 2):
        here = xp.at[slot(s, core)]
        recv(("x", s), here)
        send(("xf", s), here, here, sibling)
    recv("xs", xp.at[slot(0, 1 - core)])
    for s in (1, 3, 2):
        recv(("xf", s), xp.at[slot(s, 1 - core)])

    panel = xp[...].reshape(8 * BLOCK, 512)
    for load in loads:
        load.wait()
    paths = ((sa, ra, at_x, x), (sb, rb, at_y, y))

    def product(part, h, weight):
        for lower, width in TILES:
            term = dot(panel, weight[:, HALF * h + lower : HALF * h + lower + width], ((1,), (0,)))
            term = term.astype(BF16)
            for k in range(8):
                rows = term[BLOCK * k : BLOCK * k + BLOCK]
                bx, j = k // 2, k % 2
                if part == 0:
                    sa[bx, h, j, :, lower : lower + width] = rows
                else:
                    sb[2 * j + h, bx // 2, bx % 2, :, lower : lower + width] = rows

    def send_far(part, c):
        src, dst, at, pos = paths[part]
        send(("far", part, c), src.at[(pos + 2) % 4, c], dst.at[0, c], at(3 if c == 0 else 1))

    def send_direct(part, c):
        src, dst, at, pos = paths[part]
        step = 1 if c == 0 else 3
        send(("direct", part, c), src.at[(pos + step) % 4, c], dst.at[1, c], at(step))

    product(0, 0, wg)
    send_far(0, 0)
    product(0, 1, wg)
    send_far(0, 1)
    product(1, 0, wu)
    product(1, 1, wu)
    send_far(1, 0)
    send_far(1, 1)
    for c in (0, 1):
        send_direct(0, c)

    for s in (1, 3, 2):
        e = OFFSETS.index(4 - s)
        theirs = pl.ds(pl.multiple_of(((dep + s) % 4) * 128, 128), 128)
        send(("xw", e), xp.at[:, :, theirs], xw.at[e, :, :, pl.ds(0, 128)], at_dep(s))
    mine = pl.ds(pl.multiple_of(dep * 128, 128), 128)
    xw[0, :, :, 0:128] = xp[:, :, mine]

    for part in (0, 1):
        for c in (0, 1):
            src, dst, at, pos = paths[part]
            step = 3 if c == 0 else 1
            target = (pos + step) % 4
            recv(("far", part, c), dst.at[0, c])
            src[target, c] = (src[target, c].astype(F32) + dst[0, c].astype(F32)).astype(BF16)
            send(("sum", part, c), src.at[target, c], dst.at[2, c], at(step))
            if part == 0:
                send_direct(1, c)

    second = ((ta, rta, at_y, y), (tb, rtb, at_x, x))
    for part in (0, 1):
        src, dst, at, pos = paths[part]
        t, rt, at2, pos2 = second[part]
        for c in (0, 1):
            recv(("direct", part, c), dst.at[1, c])
            recv(("sum", part, c), dst.at[2, c])
            for j in (0, 1):
                total = (
                    src[pos, c, j].astype(F32) + dst[1, c, j].astype(F32) + dst[2, c, j].astype(F32)
                )
                t[2 * j + c if part == 0 else 2 * c + j] = total.astype(BF16)
        for s in (2, 1, 3):
            send(("two", part, s), t.at[(pos2 + s) % 4], rt.at[s - 1], at2(s))
    sums = []
    for part in (0, 1):
        t, rt, at2, pos2 = second[part]
        total = t[pos2].astype(F32)
        for s in (1, 3, 2):
            recv(("two", part, s), rt.at[s - 1])
            total = total + rt[s - 1].astype(F32)
        sums.append(total)
    gate_sum, up_sum = sums

    recv("cot", cb.at[1 - half])
    cot_wide = cb[...].reshape(BLOCK, HALF)
    gate_sig = jax.nn.sigmoid(gate_sum)
    near[0, half, x, part_here] = (
        cot_wide * up_sum * gate_sig * (1.0 + gate_sum * (1.0 - gate_sig))
    ).astype(BF16)
    near[1, half, x, part_here] = (cot_wide * gate_sum * gate_sig).astype(BF16)

    ring_one = (at_y, at_x)
    ring_two = (at_x, at_y)
    own = [near.at[part, half, x, part_here] for part in (0, 1)]
    for part in (0, 1):
        for s in (2, 1, 3):
            send(("g1", part, s), own[part], own[part], ring_one[part](s))

    mine = near.at[part_here, half, x, part_here]
    cross = near.at[1 - part_here, half, x, part_here]
    for s in (1, 3):
        e = OFFSETS.index(4 - s)
        there = others.at[e - 1, x, part_here]
        send(("zs", e), mine, there, at_dep(s))
        send(("zc", e), cross, there, at_cross(s))

    def ring_start(name, chunk, at):
        for c in (0, 1):
            ref = chunk(c, 0)
            send((name, 1, c), ref, ref, at(1))
            ref = chunk(1 - c, 0)
            send((name, 3, 1 - c), ref, ref, at(3))

    def ring_relay(name, chunk, at):
        for s, c in ((1, 0), (3, 1)):
            ref = chunk(c, 4 - s)
            recv((name, s, c), ref)
            send((name, "far", c), ref, ref, at(s))

    def ring_finish(name, chunk):
        for s, c in ((1, 1), (3, 0)):
            recv((name, s, c), chunk(c, 4 - s))
        for c in (0, 1):
            recv((name, "far", c), chunk(c, 2))

    def gate_chunk(c, step):
        return near.at[0, c, (x + step) % 4]

    def up_chunk(c, step):
        py = (y + step) % 4
        return near.at[1, py % 2, pl.ds(2 * c, 2), py // 2]

    chunks = (gate_chunk, up_chunk)

    def other_chunk(e):
        return lambda c, step: others.at[e - 1, (x + step) % 4, c]

    for part in (0, 1):
        for s in (1, 3, 2):
            recv(("g1", part, s), own[part])
        ring_start(("g2", part), chunks[part], ring_two[part])
    for part in (0, 1):
        ring_relay(("g2", part), chunks[part], ring_two[part])

    for e in (1, 2, 3):
        recv(("xw", e), xw.at[e, :, :, pl.ds(0, 128)])

    def features(s, which):
        return xw.at[:, pl.ds(4 * which, 4), :, pl.ds(128 * s, 128)]

    for s in (2, 1, 3):
        send(("xy", 4 - s), features(0, core), features(4 - s, core), at_y(s))

    for e, s in ((1, 3), (2, 1)):
        recv(("zs", e), others.at[e - 1, x, part_here])
        recv(("zc", e), others.at[e - 1, x, 1 - part_here])
        c = e - 1
        send(("zf", c), others.at[e - 1, x, c], others.at[2, x, c], at_dep(s))
        ring_start(("o", e), other_chunk(e), at_x)

    for part in (0, 1):
        ring_finish(("g2", part), chunks[part])
    total = None
    for part, weight in ((0, wg), (1, wu)):
        for h in (0, 1):
            block = near[part, h].reshape(8 * BLOCK, HALF)
            term = dot(block, weight[:, HALF * h : HALF * h + HALF], ((1,), (1,)))
            total = term if total is None else total + term
    igs[...] = total.astype(BF16).reshape(8, BLOCK, 512)

    for e in (1, 2):
        ring_relay(("o", e), other_chunk(e), at_x)
    for s in (1, 3, 2):
        recv(("xy", s), features(s, core))
        send(("xyf", s), features(s, core), features(s, core), sibling)
    for s in (1, 3, 2):
        recv(("xyf", s), features(s, 1 - core))

    def accumulate(e):
        left = xw[e].reshape(8 * BLOCK, 512)
        for lower, width in TILES:
            lanes = slice(lower, lower + width)
            if e == 0:
                block = near[part_here, half, :, :, :, lanes].reshape(8 * BLOCK, width)
                acc[:, lanes] = dot(left, block, ((0,), (0,)))
            else:
                block = others[e - 1, :, :, :, lanes].reshape(8 * BLOCK, width)
                acc[:, lanes] += dot(left, block, ((0,), (0,)))

    accumulate(0)

    for c in (0, 1):
        recv(("zf", c), others.at[2, x, c])
    ring_start(("o", 3), other_chunk(3), at_x)
    for s in range(1, 8):
        send(("ig", s), igs.at[(col + s) % 8], igr.at[s - 1], at_col(s))

    ring_finish(("o", 1), other_chunk(1))
    accumulate(1)
    ring_relay(("o", 3), other_chunk(3), at_x)
    ring_finish(("o", 2), other_chunk(2))
    accumulate(2)
    ring_finish(("o", 3), other_chunk(3))

    loss_scale = 1.0 / math.sqrt(4 * 8 * BLOCK)
    block = others[2].reshape(8 * BLOCK, HALF)
    for s in (2, 1, 3, 0):
        left = xw[3, :, :, 128 * s : 128 * s + 128].reshape(8 * BLOCK, 128)
        rows = acc[128 * s : 128 * s + 128] + dot(left, block, ((0,), (0,)))
        rows = (loss_scale * rows).astype(BF16)
        if s == 0:
            fin[y] = rows
        else:
            outs[s - 1] = rows
            send(("out", s), outs.at[s - 1], fin.at[y], at_y(s))

    total = igs[col].astype(F32)
    for s in range(1, 8):
        recv(("ig", s), igr.at[s - 1])
        total = total + igr[s - 1].astype(F32)
    ig_out[...] = total.astype(BF16)

    for s in (1, 3, 2):
        recv(("out", s), fin.at[(y + 4 - s) % 4])
    for h in (0, 1):
        gate_out[:, HALF * h : HALF * h + HALF] = fin[h]
        up_out[:, HALF * h : HALF * h + HALF] = fin[2 + h]

    for c in pending:
        c.wait_send()


def local(inputs, gate_weight, up_weight, cotangent):
    vmem = pl.BlockSpec(memory_space=pltpu.VMEM)
    hbm = pl.BlockSpec(memory_space=pl.ANY)
    return pl.pallas_call(
        kernel,
        name="swiglu_backward",
        out_shape=(
            jax.ShapeDtypeStruct((48, 512), BF16),
            jax.ShapeDtypeStruct((128, 1792), BF16),
            jax.ShapeDtypeStruct((128, 1792), BF16),
        ),
        in_specs=[vmem, hbm, hbm, vmem],
        out_specs=(vmem, vmem, vmem),
        scratch_shapes=[
            pltpu.VMEM((512, 1792), BF16),
            pltpu.VMEM((512, 1792), BF16),
            pltpu.VMEM((8, BLOCK, 512), BF16),
            pltpu.VMEM((4, 8, BLOCK, 512), BF16),
            pltpu.VMEM((4, 2, 2, BLOCK, HALF), BF16),
            pltpu.VMEM((4, 2, 2, BLOCK, HALF), BF16),
            pltpu.VMEM((3, 2, 2, BLOCK, HALF), BF16),
            pltpu.VMEM((3, 2, 2, BLOCK, HALF), BF16),
            pltpu.VMEM((4, BLOCK, HALF), BF16),
            pltpu.VMEM((4, BLOCK, HALF), BF16),
            pltpu.VMEM((3, BLOCK, HALF), BF16),
            pltpu.VMEM((3, BLOCK, HALF), BF16),
            pltpu.VMEM((2, 24, HALF), F32),
            pltpu.VMEM((2, 24, HALF), F32),
            pltpu.VMEM((2, 2, 4, 2, BLOCK, HALF), BF16),
            pltpu.VMEM((3, 4, 2, BLOCK, HALF), BF16),
            pltpu.VMEM((512, HALF), F32),
            pltpu.VMEM((3, 128, HALF), BF16),
            pltpu.VMEM((4, 128, HALF), BF16),
            pltpu.VMEM((8, BLOCK, 512), BF16),
            pltpu.VMEM((7, BLOCK, 512), BF16),
            pltpu.SemaphoreType.DMA((CHANNELS,)),
            pltpu.SemaphoreType.DMA((CHANNELS,)),
            pltpu.SemaphoreType.DMA((2,)),
        ],
        compiler_params=pltpu.CompilerParams(
            collective_id=0, has_side_effects=True, vmem_limit_bytes=56 * 2**20
        ),
    )(inputs, gate_weight, up_weight, cotangent)


def solution(mesh):
    return jax.shard_map(
        local,
        mesh=mesh,
        in_specs=(
            P(("dep", "col"), "row"),
            P("row", "col"),
            P("row", "col"),
            P(("dep", "row"), "col"),
        ),
        out_specs=(P(("dep", "col"), "row"), P(("row", "dep"), "col"), P(("row", "dep"), "col")),
        check_vma=False,
    )
```

```python
import math

import jax
import jax.numpy as jnp
from jax import lax
from jax.experimental import pallas as pl
from jax.experimental.pallas import tpu as pltpu
from jax.sharding import PartitionSpec as P

MESH = pl.DeviceIdType.MESH
F32 = jnp.float32
BF16 = jnp.bfloat16

OFFSETS = (0, 1, 3, 2)
HALF = 896
BLOCK = 48
TILES = ((0, 256), (256, 256), (512, 256), (768, 128))
CHUNKS = ((0, 512), (512, 384))
CHANNELS = 176


def dot(left, right, dims):
    return lax.dot_general(left, right, (dims, ((), ())), preferred_element_type=F32)


def kernel(
    x_in, wg_hbm, wu_hbm, cot,
    ig_out, fin_out,
    wg, wu, xp, xw, sa, sb, ra, rb, ta, tb, rta, rtb, cf, cb, near, others, acc, outs, fin, igs, igr,
    send_sem, recv_sem, local_sem,
):
    row, col, dep = lax.axis_index("row"), lax.axis_index("col"), lax.axis_index("dep")
    x, y = row // 4, row % 4
    zl, core = col // 2, col % 2
    half, part_here = y % 2, y // 2

    loads = [
        pltpu.make_async_copy(wg_hbm, wg, local_sem.at[0]),
        pltpu.make_async_copy(wu_hbm, wu, local_sem.at[1]),
    ]
    for load in loads:
        load.start()

    def at_x(step):
        return (((x + step) % 4) * 4 + y, col, dep)

    def at_y(step):
        return (x * 4 + (y + step) % 4, col, dep)

    def at_dep(step):
        return (row, col, (dep + step) % 4)

    def at_cross(step):
        return (x * 4 + (y + 2) % 4, col, (dep + step) % 4)

    def at_col(step):
        return (row, (col + step) % 8, dep)

    sibling = (row, zl * 2 + 1 - core, dep)

    barrier = pltpu.get_barrier_semaphore()
    partners = (
        [at_dep(s) for s in (2, 1, 3)]
        + [at_cross(s) for s in (1, 3)]
        + [at_col(s) for s in range(1, 8)]
        + [at_x(s) for s in (1, 2, 3)]
        + [at_y(s) for s in (1, 2, 3)]
    )
    for partner in partners:
        pl.semaphore_signal(barrier, inc=1, device_id=partner, device_id_type=MESH)
    wide = cot[...].astype(F32)
    cf[0] = wide[:, :HALF]
    cf[1] = wide[:, HALF:]
    cb[half] = cf[half]
    xp[col] = x_in[...]
    pl.semaphore_wait(barrier, len(partners))

    pending = []
    used = {}

    def channel(name):
        if name not in used:
            used[name] = len(used)
        assert len(used) <= CHANNELS
        return used[name]

    def copy(name, src, dst, device):
        i = channel(name)
        return pltpu.make_async_remote_copy(
            src_ref=src, dst_ref=dst, send_sem=send_sem.at[i], recv_sem=recv_sem.at[i],
            device_id=device, device_id_type=MESH,
        )

    def send(name, src, dst, device):
        c = copy(name, src, dst, device)
        c.start()
        pending.append(c)

    def recv(name, dst):
        copy(name, dst, dst, sibling).wait_recv()

    def slot(step, which):
        return ((zl + 4 - step) % 4) * 2 + which

    for s in (1, 2, 3):
        send(("x", s), x_in, xp.at[col], (row, ((zl + s) % 4) * 2 + core, dep))
    send("xs", x_in, xp.at[col], sibling)
    send("cot", cf.at[1 - half], cb.at[half], (x * 4 + y + 1 - 2 * half, col, dep))

    for s in (1, 3, 2):
        here = xp.at[slot(s, core)]
        recv(("x", s), here)
        send(("xf", s), here, here, sibling)
    recv("xs", xp.at[slot(0, 1 - core)])
    for s in (1, 3, 2):
        recv(("xf", s), xp.at[slot(s, 1 - core)])

    panel = xp[...].reshape(8 * BLOCK, 512)
    for load in loads:
        load.wait()
    paths = ((sa, ra, at_x, x), (sb, rb, at_y, y))

    def product(part, h, weight):
        for lower, width in TILES:
            lanes = pl.ds(pl.multiple_of(HALF * h + lower, 128), width)
            term = dot(panel, weight[:, lanes], ((1,), (0,))).astype(BF16)
            for k in range(8):
                rows = term[BLOCK * k : BLOCK * k + BLOCK]
                bx, j = k // 2, k % 2
                if part == 0:
                    sa[bx, h, j, :, lower : lower + width] = rows
                else:
                    sb[2 * j + h, bx // 2, bx % 2, :, lower : lower + width] = rows

    def send_far(part, c):
        src, dst, at, pos = paths[part]
        for j in (0, 1):
            there = at(3 if c == 0 else 1)
            send(("far", part, c, j), src.at[(pos + 2) % 4, c, j], dst.at[0, c, j], there)

    def send_direct(part, c):
        src, dst, at, pos = paths[part]
        step = 1 if c == 0 else 3
        send(("direct", part, c), src.at[(pos + step) % 4, c], dst.at[1, c], at(step))

    product(0, 0, wg)
    send_far(0, 0)
    product(1, half, wu)
    send_far(1, 0)
    send_far(1, 1)
    product(0, 1, wg)
    send_far(0, 1)
    product(1, 1 - half, wu)
    for c in (0, 1):
        send_direct(0, c)

    for s in (1, 3, 2):
        e = OFFSETS.index(4 - s)
        theirs = pl.ds(pl.multiple_of(((dep + s) % 4) * 128, 128), 128)
        send(("xw", e), xp.at[:, :, theirs], xw.at[e, :, :, pl.ds(0, 128)], at_dep(s))
    mine = pl.ds(pl.multiple_of(dep * 128, 128), 128)
    xw[0, :, :, 0:128] = xp[:, :, mine]

    for part, c, j in ((0, 0, 0), (1, 0, 0), (1, 1, 0), (0, 0, 1), (0, 1, 0), (1, 0, 1), (1, 1, 1), (0, 1, 1)):
        src, dst, at, pos = paths[part]
        step = 3 if c == 0 else 1
        target = (pos + step) % 4
        recv(("far", part, c, j), dst.at[0, c, j])
        src[target, c, j] = (src[target, c, j].astype(F32) + dst[0, c, j].astype(F32)).astype(BF16)
        send(("sum", part, c, j), src.at[target, c, j], dst.at[2, c, j], at(step))
        if part == 1 and j == 0:
            send_direct(1, c)

    second = ((ta, rta, at_y, y), (tb, rtb, at_x, x))
    for part in (0, 1):
        src, dst, at, pos = paths[part]
        t, rt, at2, pos2 = second[part]
        for c in (0, 1):
            recv(("direct", part, c), dst.at[1, c])
            for j in (0, 1):
                recv(("sum", part, c, j), dst.at[2, c, j])
                total = (
                    src[pos, c, j].astype(F32) + dst[1, c, j].astype(F32) + dst[2, c, j].astype(F32)
                )
                t[2 * j + c if part == 0 else 2 * c + j] = total.astype(BF16)
        for s in (2, 1, 3):
            send(("two", part, s), t.at[(pos2 + s) % 4], rt.at[s - 1], at2(s))
    sums = []
    for part in (0, 1):
        t, rt, at2, pos2 = second[part]
        total = t[pos2].astype(F32)
        for s in (1, 3, 2):
            recv(("two", part, s), rt.at[s - 1])
            total = total + rt[s - 1].astype(F32)
        sums.append(total)
    gate_sum, up_sum = sums

    recv("cot", cb.at[1 - half])
    cot_wide = cb[...].reshape(BLOCK, HALF)
    gate_sig = jax.nn.sigmoid(gate_sum)
    near[0, half, x, part_here] = (
        cot_wide * up_sum * gate_sig * (1.0 + gate_sum * (1.0 - gate_sig))
    ).astype(BF16)
    near[1, half, x, part_here] = (cot_wide * gate_sum * gate_sig).astype(BF16)

    ring_one = (at_y, at_x)
    ring_two = (at_x, at_y)
    own = [near.at[part, half, x, part_here] for part in (0, 1)]
    for part in (0, 1):
        for s in (2, 1, 3):
            send(("g1", part, s), own[part], own[part], ring_one[part](s))

    mine = near.at[part_here, half, x, part_here]
    cross = near.at[1 - part_here, half, x, part_here]
    for s in (1, 3):
        e = OFFSETS.index(4 - s)
        there = others.at[e - 1, x, part_here]
        send(("zs", e), mine, there, at_dep(s))
        send(("zc", e), cross, there, at_cross(s))

    def ring_start(name, chunk, at):
        for c in (0, 1):
            ref = chunk(c, 0)
            send((name, 1, c), ref, ref, at(1))
            ref = chunk(1 - c, 0)
            send((name, 3, 1 - c), ref, ref, at(3))

    def ring_relay(name, chunk, at):
        for s, c in ((1, 0), (3, 1)):
            ref = chunk(c, 4 - s)
            recv((name, s, c), ref)
            send((name, "far", c), ref, ref, at(s))

    def ring_finish(name, chunk):
        for s, c in ((1, 1), (3, 0)):
            recv((name, s, c), chunk(c, 4 - s))
        for c in (0, 1):
            recv((name, "far", c), chunk(c, 2))

    def gate_chunk(c, step):
        return near.at[0, c, (x + step) % 4]

    def up_chunk(c, step):
        py = (y + step) % 4
        return near.at[1, py % 2, pl.ds(2 * c, 2), py // 2]

    chunks = (gate_chunk, up_chunk)

    def other_chunk(e, lower=0, width=HALF):
        return lambda c, step: others.at[e - 1, (x + step) % 4, c, :, pl.ds(lower, width)]

    for part in (0, 1):
        for s in (1, 3, 2):
            recv(("g1", part, s), own[part])
        ring_start(("g2", part), chunks[part], ring_two[part])
    for part in (0, 1):
        ring_relay(("g2", part), chunks[part], ring_two[part])

    for e in (1, 2, 3):
        recv(("xw", e), xw.at[e, :, :, pl.ds(0, 128)])

    def features(s, which):
        return xw.at[:, pl.ds(4 * which, 4), :, pl.ds(128 * s, 128)]

    for s in (2, 1, 3):
        send(("xy", 4 - s), features(0, core), features(4 - s, core), at_y(s))

    for e in (1, 2):
        recv(("zs", e), others.at[e - 1, x, part_here])
        recv(("zc", e), others.at[e - 1, x, 1 - part_here])
    for lower, width in CHUNKS:
        for e, s in ((1, 3), (2, 1)):
            lanes = pl.ds(lower, width)
            c = e - 1
            send(("zf", c, lower), others.at[e - 1, x, c, :, lanes], others.at[2, x, c, :, lanes], at_dep(s))
    for e in (1, 2):
        ring_start(("o", e), other_chunk(e), at_x)

    for part in (0, 1):
        ring_finish(("g2", part), chunks[part])
    for e in (1, 2):
        ring_relay(("o", e), other_chunk(e), at_x)

    def accumulate(e):
        left = xw[e].reshape(8 * BLOCK, 512)
        for lower, width in TILES:
            lanes = slice(lower, lower + width)
            if e == 0:
                block = near[part_here, half, :, :, :, lanes].reshape(8 * BLOCK, width)
                acc[:, lanes] = dot(left, block, ((0,), (0,)))
            else:
                block = others[e - 1, :, :, :, lanes].reshape(8 * BLOCK, width)
                acc[:, lanes] += dot(left, block, ((0,), (0,)))

    for lower, width in CHUNKS:
        for c in (0, 1):
            recv(("zf", c, lower), others.at[2, x, c, :, pl.ds(lower, width)])
        ring_start(("o", 3, lower), other_chunk(3, lower, width), at_x)

    total = None
    for part, weight in ((0, wg), (1, wu)):
        for h in (0, 1):
            block = near[part, h].reshape(8 * BLOCK, HALF)
            term = dot(block, weight[:, HALF * h : HALF * h + HALF], ((1,), (1,)))
            total = term if total is None else total + term
    igs[...] = total.astype(BF16).reshape(8, BLOCK, 512)
    for s in range(1, 8):
        send(("ig", s), igs.at[(col + s) % 8], igr.at[s - 1], at_col(s))

    for s in (1, 3, 2):
        recv(("xy", s), features(s, core))
        send(("xyf", s), features(s, core), features(s, core), sibling)
    for lower, width in CHUNKS:
        ring_relay(("o", 3, lower), other_chunk(3, lower, width), at_x)
    for s in (1, 3, 2):
        recv(("xyf", s), features(s, 1 - core))
    accumulate(0)
    ring_finish(("o", 1), other_chunk(1))
    accumulate(1)
    ring_finish(("o", 2), other_chunk(2))
    accumulate(2)

    loss_scale = 1.0 / math.sqrt(4 * 8 * BLOCK)
    for lower, width in CHUNKS:
        ring_finish(("o", 3, lower), other_chunk(3, lower, width))
        lanes = pl.ds(lower, width)
        block = others[2, :, :, :, lanes].reshape(8 * BLOCK, width)
        for s in (2, 1, 3, 0):
            left = xw[3, :, :, 128 * s : 128 * s + 128].reshape(8 * BLOCK, 128)
            rows = acc[128 * s : 128 * s + 128, lanes] + dot(left, block, ((0,), (0,)))
            rows = (loss_scale * rows).astype(BF16)
            if s == 0:
                fin[y, :, lanes] = rows
            else:
                outs[s - 1, :, lanes] = rows
                send(("out", s, lower), outs.at[s - 1, :, lanes], fin.at[y, :, lanes], at_y(s))

    total = igs[col].astype(F32)
    for s in range(1, 8):
        recv(("ig", s), igr.at[s - 1])
        total = total + igr[s - 1].astype(F32)
    ig_out[...] = total.astype(BF16)

    for lower, width in CHUNKS:
        for s in (1, 3, 2):
            recv(("out", s, lower), fin.at[(y + 4 - s) % 4, :, pl.ds(lower, width)])
    fin_out[...] = fin[...]

    for c in pending:
        c.wait_send()


def write_results(input_grad, quarters, ig_out, gate_out, up_out):
    ig_out[...] = input_grad[...]
    for h in (0, 1):
        gate_out[:, HALF * h : HALF * h + HALF] = quarters[h]
        up_out[:, HALF * h : HALF * h + HALF] = quarters[2 + h]


def local(inputs, gate_weight, up_weight, cotangent):
    vmem = pl.BlockSpec(memory_space=pltpu.VMEM)
    hbm = pl.BlockSpec(memory_space=pl.ANY)
    input_grad, quarters = pl.pallas_call(
        kernel,
        name="swiglu_backward",
        out_shape=(
            jax.ShapeDtypeStruct((48, 512), BF16),
            jax.ShapeDtypeStruct((4, 128, HALF), BF16),
        ),
        in_specs=[vmem, hbm, hbm, vmem],
        out_specs=(vmem, vmem),
        scratch_shapes=[
            pltpu.VMEM((512, 1792), BF16),
            pltpu.VMEM((512, 1792), BF16),
            pltpu.VMEM((8, BLOCK, 512), BF16),
            pltpu.VMEM((4, 8, BLOCK, 512), BF16),
            pltpu.VMEM((4, 2, 2, BLOCK, HALF), BF16),
            pltpu.VMEM((4, 2, 2, BLOCK, HALF), BF16),
            pltpu.VMEM((3, 2, 2, BLOCK, HALF), BF16),
            pltpu.VMEM((3, 2, 2, BLOCK, HALF), BF16),
            pltpu.VMEM((4, BLOCK, HALF), BF16),
            pltpu.VMEM((4, BLOCK, HALF), BF16),
            pltpu.VMEM((3, BLOCK, HALF), BF16),
            pltpu.VMEM((3, BLOCK, HALF), BF16),
            pltpu.VMEM((2, 24, HALF), F32),
            pltpu.VMEM((2, 24, HALF), F32),
            pltpu.VMEM((2, 2, 4, 2, BLOCK, HALF), BF16),
            pltpu.VMEM((3, 4, 2, BLOCK, HALF), BF16),
            pltpu.VMEM((512, HALF), F32),
            pltpu.VMEM((3, 128, HALF), BF16),
            pltpu.VMEM((4, 128, HALF), BF16),
            pltpu.VMEM((8, BLOCK, 512), BF16),
            pltpu.VMEM((7, BLOCK, 512), BF16),
            pltpu.SemaphoreType.DMA((CHANNELS,)),
            pltpu.SemaphoreType.DMA((CHANNELS,)),
            pltpu.SemaphoreType.DMA((2,)),
        ],
        compiler_params=pltpu.CompilerParams(
            collective_id=0, has_side_effects=True, vmem_limit_bytes=56 * 2**20
        ),
    )(inputs, gate_weight, up_weight, cotangent)
    return pl.pallas_call(
        write_results,
        name="write_results",
        out_shape=(
            jax.ShapeDtypeStruct((48, 512), BF16),
            jax.ShapeDtypeStruct((128, 1792), BF16),
            jax.ShapeDtypeStruct((128, 1792), BF16),
        ),
        in_specs=[vmem, vmem],
        out_specs=(vmem, vmem, vmem),
    )(input_grad, quarters)


def solution(mesh):
    return jax.shard_map(
        local,
        mesh=mesh,
        in_specs=(
            P(("dep", "col"), "row"),
            P("row", "col"),
            P("row", "col"),
            P(("dep", "row"), "col"),
        ),
        out_specs=(P(("dep", "col"), "row"), P(("row", "dep"), "col"), P(("row", "dep"), "col")),
        check_vma=False,
    )
```

```python
import math

import jax
import jax.numpy as jnp
from jax import lax
from jax.experimental import pallas as pl
from jax.experimental.pallas import tpu as pltpu
from jax.sharding import PartitionSpec as P

MESH = pl.DeviceIdType.MESH
F32 = jnp.float32
BF16 = jnp.bfloat16

OFFSETS = (0, 1, 3, 2)
HALF = 896
BLOCK = 48
TILES = ((0, 256), (256, 256), (512, 256), (768, 128))
CHUNKS = ((0, 512), (512, 384))
CHANNELS = 176


def dot(left, right, dims):
    return lax.dot_general(left, right, (dims, ((), ())), preferred_element_type=F32)


def kernel(
    x_in, wg_hbm, wu_hbm, cot,
    ig_out, fin_out,
    wg, wu, xp, xw, sa, sb, ra, rb, ta, tb, rta, rtb, cf, cb, near, others, acc, outs, fin, igs, igr, xt, xc,
    send_sem, recv_sem, local_sem,
):
    row, col, dep = lax.axis_index("row"), lax.axis_index("col"), lax.axis_index("dep")
    x, y = row // 4, row % 4
    zl, core = col // 2, col % 2
    half, part_here = y % 2, y // 2

    loads = [
        pltpu.make_async_copy(wg_hbm, wg, local_sem.at[0]),
        pltpu.make_async_copy(wu_hbm, wu, local_sem.at[1]),
    ]
    for load in loads:
        load.start()

    def at_x(step):
        return (((x + step) % 4) * 4 + y, col, dep)

    def at_y(step):
        return (x * 4 + (y + step) % 4, col, dep)

    def at_dep(step):
        return (row, col, (dep + step) % 4)

    def at_col(step):
        return (row, (col + step) % 8, dep)

    sibling = (row, zl * 2 + 1 - core, dep)
    mate = (row, (zl + 1 - 2 * (zl % 2)) * 2 + core, dep)

    barrier = pltpu.get_barrier_semaphore()
    partners = (
        [at_dep(s) for s in (2, 1, 3)]
        + [at_col(s) for s in range(1, 8)]
        + [at_x(s) for s in (1, 2, 3)]
        + [at_y(s) for s in (1, 2, 3)]
    )
    for partner in partners:
        pl.semaphore_signal(barrier, inc=1, device_id=partner, device_id_type=MESH)
    wide = cot[...].astype(F32)
    cf[0] = wide[:, :HALF]
    cf[1] = wide[:, HALF:]
    cb[half] = cf[half]
    xp[col] = x_in[...]
    pl.semaphore_wait(barrier, len(partners))

    pending = []
    used = {}

    def channel(name):
        if name not in used:
            used[name] = len(used)
        assert len(used) <= CHANNELS
        return used[name]

    def copy(name, src, dst, device):
        i = channel(name)
        return pltpu.make_async_remote_copy(
            src_ref=src, dst_ref=dst, send_sem=send_sem.at[i], recv_sem=recv_sem.at[i],
            device_id=device, device_id_type=MESH,
        )

    def send(name, src, dst, device):
        c = copy(name, src, dst, device)
        c.start()
        pending.append(c)

    def recv(name, dst):
        copy(name, dst, dst, sibling).wait_recv()

    def slot(step, which):
        return ((zl + 4 - step) % 4) * 2 + which

    for s in (1, 2, 3):
        send(("x", s), x_in, xp.at[col], (row, ((zl + s) % 4) * 2 + core, dep))
    send("xs", x_in, xp.at[col], sibling)
    send("cot", cf.at[1 - half], cb.at[half], (x * 4 + y + 1 - 2 * half, col, dep))

    for s in (1, 3, 2):
        here = xp.at[slot(s, core)]
        recv(("x", s), here)
        send(("xf", s), here, here, sibling)
    recv("xs", xp.at[slot(0, 1 - core)])
    for s in (1, 3, 2):
        recv(("xf", s), xp.at[slot(s, 1 - core)])

    panel = xp[...].reshape(8 * BLOCK, 512)
    for load in loads:
        load.wait()
    paths = ((sa, ra, at_x, x), (sb, rb, at_y, y))

    def product(part, h, weight, tiles):
        for lower, width in tiles:
            lanes = pl.ds(pl.multiple_of(HALF * h + lower, 128), width)
            term = dot(panel, weight[:, lanes], ((1,), (0,))).astype(BF16)
            for k in range(8):
                rows = term[BLOCK * k : BLOCK * k + BLOCK]
                bx, j = k // 2, k % 2
                if part == 0:
                    sa[bx, h, j, :, lower : lower + width] = rows
                else:
                    sb[2 * j + h, bx // 2, bx % 2, :, lower : lower + width] = rows

    def toward(c):
        return 3 if c == 0 else 1

    def send_far(q, part, c):
        src, dst, at, pos = paths[part]
        lanes = pl.ds(*CHUNKS[q])
        there = at(toward(c))
        send(("far", q, part, c), src.at[(pos + 2) % 4, c, :, :, lanes], dst.at[0, c, :, :, lanes], there)

    def send_direct(q, part):
        src, dst, at, pos = paths[part]
        lanes = pl.ds(*CHUNKS[q])
        for c in (0, 1):
            step = 4 - toward(c)
            ref = src.at[(pos + step) % 4, c, :, :, lanes]
            send(("direct", q, part, c), ref, dst.at[1, c, :, :, lanes], at(step))

    def pass_far(q, part, c):
        src, dst, at, pos = paths[part]
        lanes = pl.ds(*CHUNKS[q])
        target = (pos + toward(c)) % 4
        recv(("far", q, part, c), dst.at[0, c, :, :, lanes])
        src[target, c, :, :, lanes] = (
            src[target, c, :, :, lanes].astype(F32) + dst[0, c, :, :, lanes].astype(F32)
        ).astype(BF16)
        ref = src.at[target, c, :, :, lanes]
        send(("sum", q, part, c), ref, dst.at[2, c, :, :, lanes], at(toward(c)))

    second = ((ta, rta, at_y, y), (tb, rtb, at_x, x))

    def start_two(q, part):
        src, dst, at, pos = paths[part]
        t, rt, at2, pos2 = second[part]
        lanes = pl.ds(*CHUNKS[q])
        for c in (0, 1):
            recv(("direct", q, part, c), dst.at[1, c, :, :, lanes])
            recv(("sum", q, part, c), dst.at[2, c, :, :, lanes])
            for j in (0, 1):
                total = (
                    src[pos, c, j, :, lanes].astype(F32)
                    + dst[1, c, j, :, lanes].astype(F32)
                    + dst[2, c, j, :, lanes].astype(F32)
                )
                t[2 * j + c if part == 0 else 2 * c + j, :, lanes] = total.astype(BF16)
        for s in (2, 1, 3):
            there = rt.at[s - 1, :, lanes]
            send(("two", q, part, s), t.at[(pos2 + s) % 4, :, lanes], there, at2(s))

    def gradients(q):
        lanes = pl.ds(*CHUNKS[q])
        sums = []
        for part in (0, 1):
            t, rt, at2, pos2 = second[part]
            total = t[pos2, :, lanes].astype(F32)
            for s in (1, 3, 2):
                recv(("two", q, part, s), rt.at[s - 1, :, lanes])
                total = total + rt[s - 1, :, lanes].astype(F32)
            sums.append(total)
        gate_sum, up_sum = sums
        cot_wide = cb[:, :, lanes].reshape(BLOCK, CHUNKS[q][1])
        gate_sig = jax.nn.sigmoid(gate_sum)
        near[0, half, x, part_here, :, lanes] = (
            cot_wide * up_sum * gate_sig * (1.0 + gate_sum * (1.0 - gate_sig))
        ).astype(BF16)
        near[1, half, x, part_here, :, lanes] = (cot_wide * gate_sum * gate_sig).astype(BF16)

    def send_groups(q):
        lanes = pl.ds(*CHUNKS[q])
        send(("swap", q), near.at[1 - part_here, half, x, part_here, :, lanes], xc.at[:, lanes], at_y(2))
        for s in (1, 3):
            e = OFFSETS.index(4 - s)
            ref = near.at[part_here, half, x, part_here, :, lanes]
            send(("zs", q, e), ref, others.at[e - 1, x, part_here, :, lanes], at_dep(s))

    def send_swapped(q):
        lanes = pl.ds(*CHUNKS[q])
        recv(("swap", q), xc.at[:, lanes])
        for s in (1, 3):
            e = OFFSETS.index(4 - s)
            ref = others.at[e - 1, x, 1 - part_here, :, lanes]
            send(("zc", q, e), xc.at[:, lanes], ref, at_dep(s))

    def pass_groups(q):
        lanes = pl.ds(*CHUNKS[q])
        for e, s in ((1, 3), (2, 1)):
            recv(("zs", q, e), others.at[e - 1, x, part_here, :, lanes])
            recv(("zc", q, e), others.at[e - 1, x, 1 - part_here, :, lanes])
            c = e - 1
            ref = others.at[e - 1, x, c, :, lanes]
            send(("zf", q, c), ref, others.at[2, x, c, :, lanes], at_dep(s))

    def ring_start(name, chunk, at):
        for c in (0, 1):
            ref = chunk(c, 0)
            send((name, 1, c), ref, ref, at(1))
            ref = chunk(1 - c, 0)
            send((name, 3, 1 - c), ref, ref, at(3))

    def ring_relay(name, chunk, at):
        for s, c in ((1, 0), (3, 1)):
            ref = chunk(c, 4 - s)
            recv((name, s, c), ref)
            send((name, "far", c), ref, ref, at(s))

    def ring_finish(name, chunk):
        for s, c in ((1, 1), (3, 0)):
            recv((name, s, c), chunk(c, 4 - s))
        for c in (0, 1):
            recv((name, "far", c), chunk(c, 2))

    def gate_chunk(lanes):
        return lambda c, step: near.at[0, c, (x + step) % 4, :, :, pl.ds(*lanes)]

    def up_chunk(lanes):
        def chunk(c, step):
            py = (y + step) % 4
            return near.at[1, py % 2, pl.ds(2 * c, 2), py // 2, :, pl.ds(*lanes)]

        return chunk

    gathers = [
        ((0, lanes, at_y, at_x, gate_chunk(lanes)), (1, lanes, at_x, at_y, up_chunk(lanes)))
        for lanes in CHUNKS
    ]

    def gather_first(q):
        for part, lanes, first, _, _ in gathers[q]:
            ref = near.at[part, half, x, part_here, :, pl.ds(*lanes)]
            for s in (2, 1, 3):
                send(("g1", q, part, s), ref, ref, first(s))

    def gather_second(q):
        for part, lanes, _, second_at, chunk in gathers[q]:
            for s in (1, 3, 2):
                recv(("g1", q, part, s), near.at[part, half, x, part_here, :, pl.ds(*lanes)])
            ring_start(("g2", q, part), chunk, second_at)

    def gather_relay(q):
        for part, _, _, second_at, chunk in gathers[q]:
            ring_relay(("g2", q, part), chunk, second_at)

    product(0, 0, wg, TILES[:2])
    send_far(0, 0, 0)
    product(1, half, wu, TILES[:2])
    send_far(0, 1, 0)
    send_far(0, 1, 1)
    product(0, 1, wg, TILES[:2])
    send_far(0, 0, 1)
    product(1, 1 - half, wu, TILES[:2])
    send_direct(0, 0)

    mine = pl.ds(4 * (zl % 2) + 2 * core, 2)
    for s in (1, 3, 2):
        e = OFFSETS.index(4 - s)
        theirs = pl.ds(pl.multiple_of(((dep + s) % 4) * 128, 128), 128)
        send(("xw", e), xp.at[mine, :, theirs], xw.at[e, mine, :, pl.ds(0, 128)], at_dep(s))
    xw[0, :, :, 0:128] = xp[:, :, pl.ds(pl.multiple_of(dep * 128, 128), 128)]

    for part, h, weight in ((0, 0, wg), (0, 1, wg), (1, 0, wu), (1, 1, wu)):
        product(part, h, weight, TILES[2:])
    for part, c in ((0, 0), (1, 0), (1, 1), (0, 1)):
        pass_far(0, part, c)
    send_direct(0, 1)
    for part, c in ((0, 0), (1, 0), (1, 1), (0, 1)):
        send_far(1, part, c)
    for part in (0, 1):
        start_two(0, part)
    send_direct(1, 0)
    for part, c in ((0, 0), (1, 0), (1, 1), (0, 1)):
        pass_far(1, part, c)
    send_direct(1, 1)
    recv("cot", cb.at[1 - half])
    gradients(0)
    send_groups(0)
    gather_first(0)
    for part in (0, 1):
        start_two(1, part)
    send_swapped(0)
    gather_second(0)
    gradients(1)
    send_groups(1)
    gather_first(1)
    gather_relay(0)
    send_swapped(1)
    gather_second(1)

    def other_chunk(e, lower=0, width=HALF):
        return lambda c, step: others.at[e - 1, (x + step) % 4, c, :, pl.ds(lower, width)]

    pass_groups(0)

    for e in (1, 2, 3):
        recv(("xw", e), xw.at[e, mine, :, pl.ds(0, 128)])

    def features(s, lz, lc):
        cols = pl.ds(4 * lz + 2 * lc, 2)
        if s == 0:
            return xw.at[pl.ds(1, 3), cols, :, pl.ds(0, 128)]
        return xw.at[:, cols, :, pl.ds(128 * s, 128)]

    lz = zl % 2
    for s in (2, 1, 3):
        src = xw.at[:, mine, :, pl.ds(0, 128)]
        send(("xy", 4 - s), src, features(4 - s, lz, core), at_y(s))

    def share(s):
        if s > 0:
            recv(("xy", s), features(s, lz, core))
        send(("xyz", s), features(s, lz, core), features(s, lz, core), mate)
        send(("xyf", s), features(s, lz, core), features(s, lz, core), sibling)

    def share_on(s):
        recv(("xyz", s), features(s, 1 - lz, core))
        send(("xyg", s), features(s, 1 - lz, core), features(s, 1 - lz, core), sibling)

    share(0)
    gather_relay(1)
    pass_groups(1)
    for e in (1, 2):
        ring_start(("o", e), other_chunk(e), at_x)

    def start_last(q):
        lower, width = CHUNKS[q]
        for c in (0, 1):
            recv(("zf", q, c), others.at[2, x, c, :, pl.ds(lower, width)])
        ring_start(("o", 3, q), other_chunk(3, lower, width), at_x)

    def accumulate(e):
        left = xt[e]
        for lower, width in TILES:
            lanes = slice(lower, lower + width)
            if e == 0:
                block = near[part_here, half, :, :, :, lanes].reshape(8 * BLOCK, width)
                acc[:, lanes] = dot(left, block, ((1,), (0,)))
            else:
                block = others[e - 1, :, :, :, lanes].reshape(8 * BLOCK, width)
                acc[:, lanes] += dot(left, block, ((1,), (0,)))

    for s in (1, 3, 2):
        share(s)
    for e in (1, 2):
        ring_relay(("o", e), other_chunk(e), at_x)
    start_last(0)
    for s in (0, 1, 3, 2):
        share_on(s)
    for q in (0, 1):
        for part, _, _, _, chunk in gathers[q]:
            ring_finish(("g2", q, part), chunk)
    start_last(1)

    total = None
    for part, weight in ((0, wg), (1, wu)):
        for h in (0, 1):
            block = near[part, h].reshape(8 * BLOCK, HALF)
            term = dot(block, weight[:, HALF * h : HALF * h + HALF], ((1,), (1,)))
            total = term if total is None else total + term
    igs[...] = total.astype(BF16).reshape(8, BLOCK, 512)
    for s in range(1, 8):
        send(("ig", s), igs.at[(col + s) % 8], igr.at[s - 1], at_col(s))

    for q, (lower, width) in enumerate(CHUNKS):
        ring_relay(("o", 3, q), other_chunk(3, lower, width), at_x)
    for s in (0, 1, 3, 2):
        recv(("xyf", s), features(s, lz, 1 - core))
        recv(("xyg", s), features(s, 1 - lz, 1 - core))
    for e in range(4):
        xt[e] = xw[e].reshape(8 * BLOCK, 512).T
    accumulate(0)
    ring_finish(("o", 1), other_chunk(1))
    accumulate(1)
    ring_finish(("o", 2), other_chunk(2))
    accumulate(2)

    loss_scale = 1.0 / math.sqrt(4 * 8 * BLOCK)
    for q, (lower, width) in enumerate(CHUNKS):
        ring_finish(("o", 3, q), other_chunk(3, lower, width))
        lanes = pl.ds(lower, width)
        block = others[2, :, :, :, lanes].reshape(8 * BLOCK, width)
        for s in (2, 1, 3, 0):
            left = xt[3, 128 * s : 128 * s + 128]
            rows = acc[128 * s : 128 * s + 128, lanes] + dot(left, block, ((1,), (0,)))
            rows = (loss_scale * rows).astype(BF16)
            if s == 0:
                fin[y, :, lanes] = rows
            else:
                outs[s - 1, :, lanes] = rows
                send(("out", s, lower), outs.at[s - 1, :, lanes], fin.at[y, :, lanes], at_y(s))

    total = igs[col].astype(F32)
    for s in range(1, 8):
        recv(("ig", s), igr.at[s - 1])
        total = total + igr[s - 1].astype(F32)
    ig_out[...] = total.astype(BF16)

    for lower, width in CHUNKS:
        for s in (1, 3, 2):
            recv(("out", s, lower), fin.at[(y + 4 - s) % 4, :, pl.ds(lower, width)])
    fin_out[...] = fin[...]

    for c in pending:
        c.wait_send()


def write_results(input_grad, quarters, ig_out, gate_out, up_out):
    ig_out[...] = input_grad[...]
    for h in (0, 1):
        gate_out[:, HALF * h : HALF * h + HALF] = quarters[h]
        up_out[:, HALF * h : HALF * h + HALF] = quarters[2 + h]


def local(inputs, gate_weight, up_weight, cotangent):
    vmem = pl.BlockSpec(memory_space=pltpu.VMEM)
    hbm = pl.BlockSpec(memory_space=pl.ANY)
    input_grad, quarters = pl.pallas_call(
        kernel,
        name="swiglu_backward",
        out_shape=(
            jax.ShapeDtypeStruct((48, 512), BF16),
            jax.ShapeDtypeStruct((4, 128, HALF), BF16),
        ),
        in_specs=[vmem, hbm, hbm, vmem],
        out_specs=(vmem, vmem),
        scratch_shapes=[
            pltpu.VMEM((512, 1792), BF16),
            pltpu.VMEM((512, 1792), BF16),
            pltpu.VMEM((8, BLOCK, 512), BF16),
            pltpu.VMEM((4, 8, BLOCK, 512), BF16),
            pltpu.VMEM((4, 2, 2, BLOCK, HALF), BF16),
            pltpu.VMEM((4, 2, 2, BLOCK, HALF), BF16),
            pltpu.VMEM((3, 2, 2, BLOCK, HALF), BF16),
            pltpu.VMEM((3, 2, 2, BLOCK, HALF), BF16),
            pltpu.VMEM((4, BLOCK, HALF), BF16),
            pltpu.VMEM((4, BLOCK, HALF), BF16),
            pltpu.VMEM((3, BLOCK, HALF), BF16),
            pltpu.VMEM((3, BLOCK, HALF), BF16),
            pltpu.VMEM((2, 24, HALF), F32),
            pltpu.VMEM((2, 24, HALF), F32),
            pltpu.VMEM((2, 2, 4, 2, BLOCK, HALF), BF16),
            pltpu.VMEM((3, 4, 2, BLOCK, HALF), BF16),
            pltpu.VMEM((512, HALF), F32),
            pltpu.VMEM((3, 128, HALF), BF16),
            pltpu.VMEM((4, 128, HALF), BF16),
            pltpu.VMEM((8, BLOCK, 512), BF16),
            pltpu.VMEM((7, BLOCK, 512), BF16),
            pltpu.VMEM((4, 512, 8 * BLOCK), BF16),
            pltpu.VMEM((BLOCK, HALF), BF16),
            pltpu.SemaphoreType.DMA((CHANNELS,)),
            pltpu.SemaphoreType.DMA((CHANNELS,)),
            pltpu.SemaphoreType.DMA((2,)),
        ],
        compiler_params=pltpu.CompilerParams(
            collective_id=0, has_side_effects=True, vmem_limit_bytes=56 * 2**20
        ),
    )(inputs, gate_weight, up_weight, cotangent)
    return pl.pallas_call(
        write_results,
        name="write_results",
        out_shape=(
            jax.ShapeDtypeStruct((48, 512), BF16),
            jax.ShapeDtypeStruct((128, 1792), BF16),
            jax.ShapeDtypeStruct((128, 1792), BF16),
        ),
        in_specs=[vmem, vmem],
        out_specs=(vmem, vmem, vmem),
    )(input_grad, quarters)


def solution(mesh):
    return jax.shard_map(
        local,
        mesh=mesh,
        in_specs=(
            P(("dep", "col"), "row"),
            P("row", "col"),
            P("row", "col"),
            P(("dep", "row"), "col"),
        ),
        out_specs=(P(("dep", "col"), "row"), P(("row", "dep"), "col"), P(("row", "dep"), "col")),
        check_vma=False,
    )
```

```python
import math

import jax
import jax.numpy as jnp
from jax import lax
from jax.experimental import pallas as pl
from jax.experimental.pallas import tpu as pltpu
from jax.sharding import PartitionSpec as P

MESH = pl.DeviceIdType.MESH
F32 = jnp.float32
BF16 = jnp.bfloat16

OFFSETS = (0, 1, 3, 2)
HALF = 896
BLOCK = 48
TILES = ((0, 256), (256, 256), (512, 256), (768, 128))
CHUNKS = ((0, 512), (512, 384))
CHANNELS = 192


def dot(left, right, dims):
    return lax.dot_general(left, right, (dims, ((), ())), preferred_element_type=F32)


def kernel(
    x_in, wg_hbm, wu_hbm, cot,
    ig_out, fin_out,
    wg, wu, xp, xw, sa, sb, ra, rb, ta, tb, rta, rtb, cf, cb, near, others, outs, fin, igs, igr, xt, xc,
    send_sem, recv_sem, local_sem,
):
    row, col, dep = lax.axis_index("row"), lax.axis_index("col"), lax.axis_index("dep")
    x, y = row // 4, row % 4
    zl, core = col // 2, col % 2
    half, part_here = y % 2, y // 2

    loads = [
        pltpu.make_async_copy(wg_hbm, wg, local_sem.at[0]),
        pltpu.make_async_copy(wu_hbm, wu, local_sem.at[1]),
    ]
    for load in loads:
        load.start()

    def at_x(step):
        return (((x + step) % 4) * 4 + y, col, dep)

    def at_y(step):
        return (x * 4 + (y + step) % 4, col, dep)

    def at_dep(step):
        return (row, col, (dep + step) % 4)

    def at_col(step):
        return (row, (col + step) % 8, dep)

    sibling = (row, zl * 2 + 1 - core, dep)
    mate = (row, (zl + 1 - 2 * (zl % 2)) * 2 + core, dep)

    barrier = pltpu.get_barrier_semaphore()
    partners = (
        [at_dep(s) for s in (2, 1, 3)]
        + [at_col(s) for s in range(1, 8)]
        + [at_x(s) for s in (1, 2, 3)]
        + [at_y(s) for s in (1, 2, 3)]
    )
    for partner in partners:
        pl.semaphore_signal(barrier, inc=1, device_id=partner, device_id_type=MESH)
    wide = cot[...].astype(F32)
    cf[0] = wide[:, :HALF]
    cf[1] = wide[:, HALF:]
    cb[half] = cf[half]
    xp[col] = x_in[...]
    pl.semaphore_wait(barrier, len(partners))

    pending = []
    used = {}

    def channel(name):
        if name not in used:
            used[name] = len(used)
        assert len(used) <= CHANNELS
        return used[name]

    def copy(name, src, dst, device):
        i = channel(name)
        return pltpu.make_async_remote_copy(
            src_ref=src, dst_ref=dst, send_sem=send_sem.at[i], recv_sem=recv_sem.at[i],
            device_id=device, device_id_type=MESH,
        )

    def send(name, src, dst, device):
        c = copy(name, src, dst, device)
        c.start()
        pending.append(c)

    def recv(name, dst):
        copy(name, dst, dst, sibling).wait_recv()

    def slot(step, which):
        return ((zl + 4 - step) % 4) * 2 + which

    for s in (1, 2, 3):
        send(("x", s), x_in, xp.at[col], (row, ((zl + s) % 4) * 2 + core, dep))
    send("xs", x_in, xp.at[col], sibling)
    send("cot", cf.at[1 - half], cb.at[half], (x * 4 + y + 1 - 2 * half, col, dep))

    for s in (1, 3, 2):
        here = xp.at[slot(s, core)]
        recv(("x", s), here)
        send(("xf", s), here, here, sibling)
    recv("xs", xp.at[slot(0, 1 - core)])
    for s in (1, 3, 2):
        recv(("xf", s), xp.at[slot(s, 1 - core)])

    panel = xp[...].reshape(8 * BLOCK, 512)
    for load in loads:
        load.wait()
    paths = ((sa, ra, at_x, x), (sb, rb, at_y, y))

    def product(part, h, weight, tiles):
        for lower, width in tiles:
            lanes = pl.ds(pl.multiple_of(HALF * h + lower, 128), width)
            term = dot(panel, weight[:, lanes], ((1,), (0,))).astype(BF16)
            for k in range(8):
                rows = term[BLOCK * k : BLOCK * k + BLOCK]
                bx, j = k // 2, k % 2
                if part == 0:
                    sa[bx, h, j, :, lower : lower + width] = rows
                else:
                    sb[2 * j + h, bx // 2, bx % 2, :, lower : lower + width] = rows

    def toward(c):
        return 3 if c == 0 else 1

    def send_far(q, part, c):
        src, dst, at, pos = paths[part]
        lanes = pl.ds(*CHUNKS[q])
        there = at(toward(c))
        send(("far", q, part, c), src.at[(pos + 2) % 4, c, :, :, lanes], dst.at[0, c, :, :, lanes], there)

    def send_direct(q, part):
        src, dst, at, pos = paths[part]
        lanes = pl.ds(*CHUNKS[q])
        for c in (0, 1):
            step = 4 - toward(c)
            ref = src.at[(pos + step) % 4, c, :, :, lanes]
            send(("direct", q, part, c), ref, dst.at[1, c, :, :, lanes], at(step))

    def pass_far(q, part, c):
        src, dst, at, pos = paths[part]
        lanes = pl.ds(*CHUNKS[q])
        target = (pos + toward(c)) % 4
        recv(("far", q, part, c), dst.at[0, c, :, :, lanes])
        src[target, c, :, :, lanes] = (
            src[target, c, :, :, lanes].astype(F32) + dst[0, c, :, :, lanes].astype(F32)
        ).astype(BF16)
        ref = src.at[target, c, :, :, lanes]
        send(("sum", q, part, c), ref, dst.at[2, c, :, :, lanes], at(toward(c)))

    second = ((ta, rta, at_y, y), (tb, rtb, at_x, x))

    def start_two(q, part):
        src, dst, at, pos = paths[part]
        t, rt, at2, pos2 = second[part]
        lanes = pl.ds(*CHUNKS[q])
        for c in (0, 1):
            recv(("direct", q, part, c), dst.at[1, c, :, :, lanes])
            recv(("sum", q, part, c), dst.at[2, c, :, :, lanes])
            for j in (0, 1):
                total = (
                    src[pos, c, j, :, lanes].astype(F32)
                    + dst[1, c, j, :, lanes].astype(F32)
                    + dst[2, c, j, :, lanes].astype(F32)
                )
                t[2 * j + c if part == 0 else 2 * c + j, :, lanes] = total.astype(BF16)
        for s in (2, 1, 3):
            there = rt.at[s - 1, :, lanes]
            send(("two", q, part, s), t.at[(pos2 + s) % 4, :, lanes], there, at2(s))

    def gradients(q):
        lanes = pl.ds(*CHUNKS[q])
        sums = []
        for part in (0, 1):
            t, rt, at2, pos2 = second[part]
            total = t[pos2, :, lanes].astype(F32)
            for s in (1, 3, 2):
                recv(("two", q, part, s), rt.at[s - 1, :, lanes])
                total = total + rt[s - 1, :, lanes].astype(F32)
            sums.append(total)
        gate_sum, up_sum = sums
        cot_wide = cb[:, :, lanes].reshape(BLOCK, CHUNKS[q][1])
        gate_sig = jax.nn.sigmoid(gate_sum)
        near[0, half, x, part_here, :, lanes] = (
            cot_wide * up_sum * gate_sig * (1.0 + gate_sum * (1.0 - gate_sig))
        ).astype(BF16)
        near[1, half, x, part_here, :, lanes] = (cot_wide * gate_sum * gate_sig).astype(BF16)

    def send_groups(q):
        lanes = pl.ds(*CHUNKS[q])
        send(("swap", q), near.at[1 - part_here, half, x, part_here, :, lanes], xc.at[:, lanes], at_y(2))
        for s in (1, 3):
            e = OFFSETS.index(4 - s)
            ref = near.at[part_here, half, x, part_here, :, lanes]
            send(("zs", q, e), ref, others.at[e - 1, x, part_here, :, lanes], at_dep(s))

    def send_swapped(q):
        lanes = pl.ds(*CHUNKS[q])
        recv(("swap", q), xc.at[:, lanes])
        for s in (1, 3):
            e = OFFSETS.index(4 - s)
            ref = others.at[e - 1, x, 1 - part_here, :, lanes]
            send(("zc", q, e), xc.at[:, lanes], ref, at_dep(s))

    def pass_groups(q):
        lanes = pl.ds(*CHUNKS[q])
        for e, s in ((1, 3), (2, 1)):
            recv(("zs", q, e), others.at[e - 1, x, part_here, :, lanes])
            recv(("zc", q, e), others.at[e - 1, x, 1 - part_here, :, lanes])
            c = e - 1
            ref = others.at[e - 1, x, c, :, lanes]
            send(("zf", q, c), ref, others.at[2, x, c, :, lanes], at_dep(s))

    def ring_start(name, chunk, at):
        for c in (0, 1):
            ref = chunk(c, 0)
            send((name, 1, c), ref, ref, at(1))
            ref = chunk(1 - c, 0)
            send((name, 3, 1 - c), ref, ref, at(3))

    def ring_relay(name, chunk, at):
        for s, c in ((1, 0), (3, 1)):
            ref = chunk(c, 4 - s)
            recv((name, s, c), ref)
            send((name, "far", c), ref, ref, at(s))

    def ring_finish(name, chunk):
        for s, c in ((1, 1), (3, 0)):
            recv((name, s, c), chunk(c, 4 - s))
        for c in (0, 1):
            recv((name, "far", c), chunk(c, 2))

    def along_x(part, lanes):
        return lambda c, step: near.at[part, c, (x + step) % 4, :, :, pl.ds(*lanes)]

    def along_y(part, lanes):
        def chunk(c, step):
            py = (y + step) % 4
            return near.at[part, py % 2, pl.ds(2 * c, 2), py // 2, :, pl.ds(*lanes)]

        return chunk

    first, last = CHUNKS
    gathers = (
        ((0, first, at_y, at_x, along_x(0, first)), (1, first, at_x, at_y, along_y(1, first))),
        ((0, last, at_x, at_y, along_y(0, last)), (1, last, at_x, at_y, along_y(1, last))),
    )

    def gather_first(q):
        for part, lanes, first_at, _, _ in gathers[q]:
            ref = near.at[part, half, x, part_here, :, pl.ds(*lanes)]
            for s in (2, 1, 3):
                send(("g1", q, part, s), ref, ref, first_at(s))

    def gather_second(q):
        for part, lanes, _, second_at, chunk in gathers[q]:
            for s in (1, 3, 2):
                recv(("g1", q, part, s), near.at[part, half, x, part_here, :, pl.ds(*lanes)])
            ring_start(("g2", q, part), chunk, second_at)

    def gather_relay(q):
        for part, _, _, second_at, chunk in gathers[q]:
            ring_relay(("g2", q, part), chunk, second_at)

    product(0, 0, wg, TILES[:2])
    send_far(0, 0, 0)
    product(1, half, wu, TILES[:2])
    send_far(0, 1, 0)
    send_far(0, 1, 1)
    product(0, 1, wg, TILES[:2])
    send_far(0, 0, 1)
    product(1, 1 - half, wu, TILES[:2])
    send_direct(0, 0)

    mine = pl.ds(4 * (zl % 2) + 2 * core, 2)
    for s in (1, 3, 2):
        e = OFFSETS.index(4 - s)
        theirs = pl.ds(pl.multiple_of(((dep + s) % 4) * 128, 128), 128)
        send(("xw", e), xp.at[mine, :, theirs], xw.at[e, mine, :, pl.ds(0, 128)], at_dep(s))
    xw[0, :, :, 0:128] = xp[:, :, pl.ds(pl.multiple_of(dep * 128, 128), 128)]

    for part, h, weight in ((0, 0, wg), (0, 1, wg), (1, 0, wu), (1, 1, wu)):
        product(part, h, weight, TILES[2:])
    for part, c in ((0, 0), (1, 0), (1, 1), (0, 1)):
        pass_far(0, part, c)
    send_direct(0, 1)
    for part, c in ((0, 0), (1, 0), (1, 1), (0, 1)):
        send_far(1, part, c)
    for part in (0, 1):
        start_two(0, part)
    send_direct(1, 0)
    for part, c in ((0, 0), (1, 0), (1, 1), (0, 1)):
        pass_far(1, part, c)
    send_direct(1, 1)
    recv("cot", cb.at[1 - half])
    gradients(0)
    send_groups(0)
    gather_first(0)
    for part in (0, 1):
        start_two(1, part)
    send_swapped(0)
    gather_second(0)
    gradients(1)
    send_groups(1)
    gather_first(1)
    gather_relay(0)
    send_swapped(1)
    gather_second(1)

    def other_chunk(e, q):
        return lambda c, step: others.at[e - 1, (x + step) % 4, c, :, pl.ds(*CHUNKS[q])]

    def others_start(q):
        for e in (1, 2):
            ring_start(("o", e, q), other_chunk(e, q), at_x)

    def others_relay(q):
        for e in (1, 2):
            ring_relay(("o", e, q), other_chunk(e, q), at_x)

    pass_groups(0)
    others_start(0)

    for e in (1, 2, 3):
        recv(("xw", e), xw.at[e, mine, :, pl.ds(0, 128)])

    def features(s, lz, lc):
        cols = pl.ds(4 * lz + 2 * lc, 2)
        if s == 0:
            return xw.at[pl.ds(1, 3), cols, :, pl.ds(0, 128)]
        return xw.at[:, cols, :, pl.ds(128 * s, 128)]

    lz = zl % 2
    for s in (2, 1, 3):
        src = xw.at[:, mine, :, pl.ds(0, 128)]
        send(("xy", 4 - s), src, features(4 - s, lz, core), at_y(s))

    def share(s):
        if s > 0:
            recv(("xy", s), features(s, lz, core))
        send(("xyz", s), features(s, lz, core), features(s, lz, core), mate)
        send(("xyf", s), features(s, lz, core), features(s, lz, core), sibling)

    def share_on(s):
        recv(("xyz", s), features(s, 1 - lz, core))
        send(("xyg", s), features(s, 1 - lz, core), features(s, 1 - lz, core), sibling)

    share(0)
    gather_relay(1)
    pass_groups(1)
    others_start(1)

    def start_last(q):
        for c in (0, 1):
            recv(("zf", q, c), others.at[2, x, c, :, pl.ds(*CHUNKS[q])])
        ring_start(("o", 3, q), other_chunk(3, q), at_x)

    def input_grad():
        for part, _, _, _, chunk in gathers[1]:
            ring_finish(("g2", 1, part), chunk)
        total = None
        for part, weight in ((0, wg), (1, wu)):
            for h in (0, 1):
                block = near[part, h].reshape(8 * BLOCK, HALF)
                term = dot(block, weight[:, HALF * h : HALF * h + HALF], ((1,), (1,)))
                total = term if total is None else total + term
        igs[...] = total.astype(BF16).reshape(8, BLOCK, 512)
        for s in range(1, 8):
            send(("ig", s), igs.at[(col + s) % 8], igr.at[s - 1], at_col(s))

    loss_scale = 1.0 / math.sqrt(4 * 8 * BLOCK)

    def weight_grads(q):
        lower, width = CHUNKS[q]
        lanes = pl.ds(lower, width)
        for e in (1, 2, 3):
            ring_finish(("o", e, q), other_chunk(e, q))
        if q == 0:
            for part, _, _, _, chunk in gathers[0]:
                ring_finish(("g2", 0, part), chunk)
        for start, count in ((1, 2), (3, 1), (0, 1)):
            rows = slice(128 * start, 128 * (start + count))
            block = near[part_here, half, :, :, :, lanes].reshape(8 * BLOCK, width)
            result = dot(xt[rows, 0:384], block, ((1,), (0,)))
            block = others[:, :, :, :, lanes].reshape(24 * BLOCK, width)
            result = result + dot(xt[rows, 384:1536], block, ((1,), (0,)))
            result = (loss_scale * result).astype(BF16)
            for s in range(start, start + count):
                piece = result[128 * (s - start) : 128 * (s - start) + 128]
                if s == 0:
                    fin[y, :, lanes] = piece
                else:
                    outs[s - 1, :, lanes] = piece
                    send(("out", s, lower), outs.at[s - 1, :, lanes], fin.at[y, :, lanes], at_y(s))

    others_relay(0)
    start_last(0)
    others_relay(1)
    for s in (1, 3, 2):
        share(s)
    start_last(1)
    ring_relay(("o", 3, 0), other_chunk(3, 0), at_x)
    for s in (0, 1, 3, 2):
        share_on(s)
    ring_relay(("o", 3, 1), other_chunk(3, 1), at_x)
    for s in (0, 1, 3, 2):
        recv(("xyf", s), features(s, lz, 1 - core))
        recv(("xyg", s), features(s, 1 - lz, 1 - core))
    for e in range(4):
        xt[:, 384 * e : 384 * e + 384] = xw[e].reshape(8 * BLOCK, 512).T
    weight_grads(0)
    input_grad()
    weight_grads(1)

    total = igs[col].astype(F32)
    for s in range(1, 8):
        recv(("ig", s), igr.at[s - 1])
        total = total + igr[s - 1].astype(F32)
    ig_out[...] = total.astype(BF16)

    for lower, width in CHUNKS:
        for s in (1, 3, 2):
            recv(("out", s, lower), fin.at[(y + 4 - s) % 4, :, pl.ds(lower, width)])
    fin_out[...] = fin[...]

    for c in pending:
        c.wait_send()


def write_results(input_grad, quarters, ig_out, gate_out, up_out):
    ig_out[...] = input_grad[...]
    for h in (0, 1):
        gate_out[:, HALF * h : HALF * h + HALF] = quarters[h]
        up_out[:, HALF * h : HALF * h + HALF] = quarters[2 + h]


def local(inputs, gate_weight, up_weight, cotangent):
    vmem = pl.BlockSpec(memory_space=pltpu.VMEM)
    hbm = pl.BlockSpec(memory_space=pl.ANY)
    input_grad, quarters = pl.pallas_call(
        kernel,
        name="swiglu_backward",
        out_shape=(
            jax.ShapeDtypeStruct((48, 512), BF16),
            jax.ShapeDtypeStruct((4, 128, HALF), BF16),
        ),
        in_specs=[vmem, hbm, hbm, vmem],
        out_specs=(vmem, vmem),
        scratch_shapes=[
            pltpu.VMEM((512, 1792), BF16),
            pltpu.VMEM((512, 1792), BF16),
            pltpu.VMEM((8, BLOCK, 512), BF16),
            pltpu.VMEM((4, 8, BLOCK, 512), BF16),
            pltpu.VMEM((4, 2, 2, BLOCK, HALF), BF16),
            pltpu.VMEM((4, 2, 2, BLOCK, HALF), BF16),
            pltpu.VMEM((3, 2, 2, BLOCK, HALF), BF16),
            pltpu.VMEM((3, 2, 2, BLOCK, HALF), BF16),
            pltpu.VMEM((4, BLOCK, HALF), BF16),
            pltpu.VMEM((4, BLOCK, HALF), BF16),
            pltpu.VMEM((3, BLOCK, HALF), BF16),
            pltpu.VMEM((3, BLOCK, HALF), BF16),
            pltpu.VMEM((2, 24, HALF), F32),
            pltpu.VMEM((2, 24, HALF), F32),
            pltpu.VMEM((2, 2, 4, 2, BLOCK, HALF), BF16),
            pltpu.VMEM((3, 4, 2, BLOCK, HALF), BF16),
            pltpu.VMEM((3, 128, HALF), BF16),
            pltpu.VMEM((4, 128, HALF), BF16),
            pltpu.VMEM((8, BLOCK, 512), BF16),
            pltpu.VMEM((7, BLOCK, 512), BF16),
            pltpu.VMEM((512, 32 * BLOCK), BF16),
            pltpu.VMEM((BLOCK, HALF), BF16),
            pltpu.SemaphoreType.DMA((CHANNELS,)),
            pltpu.SemaphoreType.DMA((CHANNELS,)),
            pltpu.SemaphoreType.DMA((2,)),
        ],
        compiler_params=pltpu.CompilerParams(
            collective_id=0, has_side_effects=True, vmem_limit_bytes=56 * 2**20
        ),
    )(inputs, gate_weight, up_weight, cotangent)
    return pl.pallas_call(
        write_results,
        name="write_results",
        out_shape=(
            jax.ShapeDtypeStruct((48, 512), BF16),
            jax.ShapeDtypeStruct((128, 1792), BF16),
            jax.ShapeDtypeStruct((128, 1792), BF16),
        ),
        in_specs=[vmem, vmem],
        out_specs=(vmem, vmem, vmem),
    )(input_grad, quarters)


def solution(mesh):
    return jax.shard_map(
        local,
        mesh=mesh,
        in_specs=(
            P(("dep", "col"), "row"),
            P("row", "col"),
            P("row", "col"),
            P(("dep", "row"), "col"),
        ),
        out_specs=(P(("dep", "col"), "row"), P(("row", "dep"), "col"), P(("row", "dep"), "col")),
        check_vma=False,
    )
```
